128 devices in a mesh: morton: 128 (over x, z, y, core).
Axes of the slice: x: 4, y: 4, z: 4, core: 2. Of those that a mesh axis runs over, the one named last changes fastest.
Arguments:
- charges: bfloat16 [32768, 256], P('morton'), may hold values from -6 to 6
- basis: bfloat16 [32768, 64, 256], P('morton'), may hold values from -0.75 to 0.75
- m2m_ops: bfloat16 [8, 256, 256], replicated, may hold values from -0.125 to 0.125
- l2l_ops: bfloat16 [8, 256, 256], replicated, may hold values from -0.375 to 0.375
- m2l_ops: bfloat16 [64, 256, 256], replicated, may hold values from -0.09375 to 0.09375
- send_rows: int32 [128, 8, 128], P('morton'), may hold values from 0 to 255
- vlist: int32 [32768, 64], P('morton'), may hold values from 0 to 1280
- top_list: int32 [64, 16], replicated, may hold values from 0 to 63
- top_ops: int32 [64, 16], replicated, may hold values from 0 to 63
Outputs:
- leaf_local: float32 [32768, 1024], P('morton')
The draws below stay inside these ranges and needn't reach their ends.
Inputs may be any that keep to these rules, and one draw needn't show every extreme that they name: `send_rows`: an index into the sending device's own leaves. `vlist`: rows below 256 are the device's own leaves, row 256 + j * 128 + c is slot j's c-th received leaf, row 1280 is empty.
All inputs are finite; a program needn't handle non-finite values.
Results may differ from the reference program's by a relative error of at most 0.0029.
Values may be sent and summed in bfloat16 or wider, within the bound.
No kernel may reach another device: no remote copies, remote signals or barrier semaphores. Data moves between devices by JAX's collectives and lax.ppermute only.
A program may use at most 192 MiB of HBM per device.

```python
import jax
import jax.numpy as jnp
from jax import lax

P_SIZE = 256
S = 64
K = 4
LDEV = 256
HOPS = 4
OFFS = 64
TOPL = 16
CAP = 128
TABLE = 1280
NL = 32768
TOPC = 64
N_MORTON = 128


def set_ends(drawn, rng, least, high):
    longest = drawn.shape.index(max(drawn.shape))
    spots = []
    for shift in (0, 1):
        where = [jax.random.randint(jax.random.fold_in(rng, axis), (), 0, length) for axis, length in enumerate(drawn.shape)]
        where[longest] = (where[longest] + shift) % drawn.shape[longest]
        spots.append(tuple(where))
    return drawn.at[spots[0]].set(least).at[spots[1]].set(high)


def steps_of(key, dims, split, low, largest):
    gain = 1.0
    for position, shards_of in split:
        draws = jax.random.uniform(jax.random.fold_in(jax.random.fold_in(key, 6), position), (shards_of,), jnp.float32, low / len(split), largest / len(split))
        gain = gain * jnp.repeat(jnp.exp(draws), dims[position] // shards_of).reshape((-1,) + (1,) * (len(dims) - 1 - position))
    return gain


def normal_values(own_key, extent, deviation, bound, pieces=(), kind=jnp.bfloat16):
    result = jax.random.normal(own_key, extent, jnp.float32) * deviation
    if len(pieces) > 0:
        result = steps_of(own_key, extent, pieces, -0.22, 0.18) * result
    return jnp.clip(result, min=-bound, max=bound).astype(kind)


def setup_inputs(seed: int = 0) -> dict:
    key_list = jax.random.split(jax.random.key(seed), 10)
    return {
        "charges": normal_values(key_list[0], (NL, K * S), 1.0, 6.0, ((0, 128),)),
        "basis": normal_values(key_list[1], (NL, S, P_SIZE), S ** -0.5, 0.75, ((0, 128),)),
        "m2m_ops": normal_values(key_list[2], (8, P_SIZE, P_SIZE), (8 * P_SIZE) ** -0.5, 0.125),
        "l2l_ops": normal_values(key_list[3], (8, P_SIZE, P_SIZE), P_SIZE ** -0.5, 0.375),
        "m2l_ops": normal_values(key_list[4], (OFFS, P_SIZE, P_SIZE), (P_SIZE * OFFS // 4) ** -0.5, 0.09375),
        "send_rows": set_ends(jax.random.randint(key_list[5], (N_MORTON, 2 * HOPS, CAP), 0, LDEV), jax.random.fold_in(key_list[5], 1), 0, LDEV - 1).astype(jnp.int32),
        "vlist": set_ends(jax.random.randint(key_list[6], (NL, OFFS), 0, TABLE + 1), jax.random.fold_in(key_list[6], 1), 0, TABLE).astype(jnp.int32),
        "top_list": set_ends(jax.random.randint(key_list[7], (TOPC, TOPL), 0, TOPC), jax.random.fold_in(key_list[7], 1), 0, TOPC - 1).astype(jnp.int32),
        "top_ops": set_ends(jax.random.randint(key_list[8], (TOPC, TOPL), 0, OFFS), jax.random.fold_in(key_list[8], 1), 0, OFFS - 1).astype(jnp.int32),
    }


HIGH = lax.Precision.HIGHEST


def lift(mult, ops):
    rows = mult.reshape(mult.shape[0] // 8, 8, mult.shape[1], mult.shape[2])
    return jnp.einsum("nckp,cpq->nkq", rows, ops, precision=HIGH)


def lower(local, ops):
    spread = jnp.einsum("nkp,cpq->nckq", local, ops, precision=HIGH)
    return spread.reshape(local.shape[0] * 8, local.shape[1], local.shape[2])


def reference(charges, basis, m2m_ops, l2l_ops, m2l_ops, send_rows, vlist, top_list, top_ops):
    m2m_wide = m2m_ops.astype(jnp.float32)
    l2l_wide = l2l_ops.astype(jnp.float32)
    m2l_wide = m2l_ops.astype(jnp.float32)

    def moments(device):
        block_c = lax.dynamic_slice_in_dim(charges, device * LDEV, LDEV, 0).astype(jnp.float32)
        block_b = lax.dynamic_slice_in_dim(basis, device * LDEV, LDEV, 0).astype(jnp.float32)
        return jnp.einsum("lks,lsp->lkp", block_c.reshape(LDEV, K, S), block_b).astype(jnp.bfloat16)

    leaf_mult = lax.map(moments, jnp.arange(N_MORTON, dtype=jnp.int32)).reshape(NL, K, P_SIZE)
    parent_mult = lift(leaf_mult.astype(jnp.float32), m2m_wide)
    grand_mult = lift(parent_mult, m2m_wide)
    top_mult = lift(grand_mult, m2m_wide)
    top_local = jnp.einsum("tekp,tepq->tkq", top_mult[top_list], m2l_wide[top_ops], precision=HIGH)
    leaf_down = lower(lower(lower(top_local, l2l_wide), l2l_wide), l2l_wide)

    def far_field(device):
        parts = [lax.dynamic_slice_in_dim(leaf_mult, device * LDEV, LDEV, 0)]
        for hop in range(HOPS):
            for sign in (1, -1):
                slot = 2 * hop + (0 if sign == 1 else 1)
                source = device - sign * (2 ** hop)
                valid = jnp.logical_and(source >= 0, source < N_MORTON)
                safe = jnp.clip(source, 0, N_MORTON - 1).astype(jnp.int32)
                picked = send_rows[safe, slot] + safe * LDEV
                rows = jnp.take(leaf_mult, picked, axis=0)
                parts.append(jnp.where(valid, rows, jnp.zeros_like(rows)))
        parts.append(jnp.zeros((1, K, P_SIZE), jnp.bfloat16))
        table = jnp.concatenate(parts, axis=0).astype(jnp.float32)
        lists = lax.dynamic_slice_in_dim(vlist, device * LDEV, LDEV, 0)

        def group(step, total):
            cols = lax.dynamic_slice_in_dim(lists, step * 8, 8, 1)
            ops = lax.dynamic_slice_in_dim(m2l_wide, step * 8, 8, 0)
            return total + jnp.einsum("lokp,opq->lkq", jnp.take(table, cols, axis=0), ops)

        return lax.fori_loop(0, OFFS // 8, group, jnp.zeros((LDEV, K, P_SIZE), jnp.float32))

    leaf_far = lax.map(far_field, jnp.arange(N_MORTON, dtype=jnp.int32)).reshape(NL, K, P_SIZE)
    return (leaf_down + leaf_far).reshape(NL, K * P_SIZE)
```

```python
import functools

import jax
import jax.numpy as jnp
from jax import lax
from jax.experimental import pallas as pl
from jax.experimental.pallas import tpu as pltpu
from jax.sharding import PartitionSpec as P


F32 = jnp.float32
BF16 = jnp.bfloat16
VMEM = pl.BlockSpec(memory_space=pltpu.VMEM)
SMEM = pl.BlockSpec(memory_space=pltpu.SMEM)
HBM = pl.BlockSpec(memory_space=pl.ANY)

LEAVES = 256
SLOTS = 8
CAP = 128
OFFS = 64
EMPTY = LEAVES + SLOTS * CAP
STEP = 32
LB = 128
OG = 8
REACH = [2 ** (j // 2) * (1 if j % 2 == 0 else -1) for j in range(SLOTS)]


def params(mib):
    return pltpu.CompilerParams(vmem_limit_bytes=mib * 2**20)


def parts(x):
    high = x.astype(BF16)
    low = (x - high.astype(F32)).astype(BF16)
    return jnp.concatenate([high, low], axis=0)


def dot(a, b):
    return jnp.dot(a, b, preferred_element_type=F32)


def split_dot(x, w):
    y = dot(parts(x), w)
    return y[: x.shape[0]] + y[x.shape[0] :]


def leaf_kernel(rows, charges, basis, own, *rest):
    packed, (spread0, spread1, table) = rest[:SLOTS], rest[SLOTS:]
    step = pl.program_id(0)

    @pl.when(step == 0)
    def _():
        source = lax.broadcasted_iota(jnp.int32, (256, 256), 0)
        lane = lax.broadcasted_iota(jnp.int32, (256, 256), 1)
        for k in range(4):
            repeat = jnp.where(source == k * 64 + lane % 64, 1.0, 0.0).astype(BF16)
            wide = dot(charges[...], repeat)
            spread0[pl.ds(k, LEAVES, stride=4), :] = wide[:, :128]
            spread1[pl.ds(k, LEAVES, stride=4), :] = wide[:, 128:]

    row = lax.broadcasted_iota(jnp.int32, (16, 256), 0)
    lane = lax.broadcasted_iota(jnp.int32, (16, 256), 1)
    own_block = row // 4 == lane // 64
    upper = lax.broadcasted_iota(jnp.int32, (2, 8, 128), 1) < 4
    for g in range(STEP // 4):
        at = pl.ds(pl.multiple_of(step * (STEP * 4) + 16 * g, 16), 16)
        wide = jnp.concatenate([spread0[at, :], spread1[at, :]], axis=1)
        lhs = jnp.where(own_block, wide, 0.0).astype(BF16)
        res = dot(lhs, basis[256 * g : 256 * g + 256, :])
        x0 = res[:, :128].reshape(2, 8, 128)
        x1 = res[:, 128:].reshape(2, 8, 128)
        even = jnp.where(upper, x0, pltpu.roll(x1, 4, 1))
        odd = jnp.where(upper, pltpu.roll(x0, 4, 1), x1)
        tiles = jnp.concatenate([even[0], odd[0], even[1], odd[1]], axis=0)
        at = pl.ds(pl.multiple_of(step * (STEP * 8) + 32 * g, 32), 32)
        table[at, :] = tiles
        own[at, :] = tiles.astype(BF16)

    @pl.when(step == LEAVES // STEP - 1)
    def _():
        for j in range(SLOTS):

            @pl.loop(0, CAP // 16)
            def _(i):
                for c in range(0, 16, 2):
                    pair = []
                    for d in range(2):
                        leaf = rows[j, i * 16 + c + d]
                        pair.append(table[pl.ds(pl.multiple_of(leaf * 8, 8), 8), :])
                    at = pl.ds(pl.multiple_of(i * 128 + c * 8, 16), 16)
                    packed[j][at, :] = jnp.concatenate(pair, axis=0).astype(BF16)


def leaf_call(rows, charges, basis):
    tiles = jax.ShapeDtypeStruct((LEAVES * 8, 128), BF16)
    sent = jax.ShapeDtypeStruct((CAP * 8, 128), BF16)
    whole = lambda i: (0, 0)
    return pl.pallas_call(
        leaf_kernel,
        grid=(LEAVES // STEP,),
        out_shape=[tiles] + [sent] * SLOTS,
        in_specs=[
            SMEM,
            pl.BlockSpec((LEAVES, 256), whole),
            pl.BlockSpec((STEP * 64, 256), lambda i: (i, 0)),
        ],
        out_specs=[pl.BlockSpec((LEAVES * 8, 128), whole)]
        + [pl.BlockSpec((CAP * 8, 128), whole)] * SLOTS,
        scratch_shapes=[
            pltpu.VMEM((LEAVES * 4, 128), F32),
            pltpu.VMEM((LEAVES * 4, 128), F32),
            pltpu.VMEM((LEAVES * 8, 128), F32),
        ],
        compiler_params=params(32),
        name="leaf",
    )(rows, charges, basis)


def up_kernel(device, own, ops, out, wide, p0, p1, g0, g1):
    wide[...] = own[...].astype(F32)
    total = jnp.zeros((128, 256), F32)
    for c in range(8):
        blocks = []
        for k in range(4):
            halves = [wide[pl.ds(8 * c + 4 * h + k, 32, stride=64), :] for h in range(2)]
            blocks.append(jnp.concatenate(halves, axis=1))
        total = total + dot(jnp.concatenate(blocks, axis=0).astype(BF16), ops[c])
    p0[...] = total[:, :128]
    p1[...] = total[:, 128:]
    total = jnp.zeros((16, 256), F32)
    for c in range(8):
        at = pl.ds(c, 16, stride=8)
        total = total + split_dot(jnp.concatenate([p0[at, :], p1[at, :]], axis=1), ops[c])
    octant = lax.rem(device[0], 2) * 4
    child = lax.broadcasted_iota(jnp.int32, (16, 256), 0) % 4
    spread = jnp.zeros((16, 256), F32)
    for g in range(4):
        spread = spread + split_dot(jnp.where(child == g, total, 0.0), ops[octant + g])
    g0[...] = spread[:, :128]
    g1[...] = spread[:, 128:]
    for h, half in enumerate((g0, g1)):
        piece = [half[pl.ds(g, 4, stride=4), :] for g in range(4)]
        out[4 * h : 4 * h + 4, :] = (piece[0] + piece[1]) + (piece[2] + piece[3])


def up_call(device, own, ops):
    return pl.pallas_call(
        up_kernel,
        out_shape=jax.ShapeDtypeStruct((8, 128), F32),
        in_specs=[SMEM, VMEM, VMEM],
        out_specs=VMEM,
        scratch_shapes=[
            pltpu.VMEM((LEAVES * 8, 128), F32),
            pltpu.VMEM((128, 128), F32),
            pltpu.VMEM((128, 128), F32),
            pltpu.VMEM((16, 128), F32),
            pltpu.VMEM((16, 128), F32),
        ],
        compiler_params=params(16),
        name="up",
    )(device, own, ops)


def down_kernel(device, top_list, top_ops, pieces, far_ops, ops, out, chosen, g0, g1, p0, p1, sems):
    cell = device[0] // 2

    def fetch(e):
        return pltpu.make_async_copy(far_ops.at[top_ops[cell, e]], chosen.at[e], sems.at[e])

    for e in range(16):
        fetch(e).start()
    low = jnp.zeros((8, 256), F32)
    high = jnp.zeros((8, 256), F32)
    for e in range(16):
        t = top_list[cell, e]
        lhs = pieces[2 * t] + pieces[2 * t + 1]
        fetch(e).wait()
        low = low + split_dot(lhs, chosen[e, 0])
        high = high + split_dot(lhs, chosen[e, 1])
    top = low + pltpu.roll(high, 4, 0)
    octant = lax.rem(device[0], 2) * 4
    for g in range(4):
        res = split_dot(top, ops[octant + g])
        g0[pl.ds(g, 4, stride=4), :] = res[:4, :128]
        g1[pl.ds(g, 4, stride=4), :] = res[:4, 128:]
    grand = parts(jnp.concatenate([g0[...], g1[...]], axis=1))
    for c in range(8):
        res = dot(grand, ops[c])
        res = res[:16] + res[16:]
        p0[pl.ds(c, 16, stride=8), :] = res[:, :128]
        p1[pl.ds(c, 16, stride=8), :] = res[:, 128:]
    parent = parts(jnp.concatenate([p0[...], p1[...]], axis=1))
    for c in range(8):
        res = dot(parent, ops[c])
        res = res[:128] + res[128:]
        for k in range(4):
            for h in range(2):
                at = pl.ds((4 * h + k) * LEAVES + c, 32, stride=8)
                out[at, :] = res[32 * k : 32 * k + 32, 128 * h : 128 * h + 128]


def down_call(device, top_list, top_ops, pieces, far_ops, ops):
    return pl.pallas_call(
        down_kernel,
        out_shape=jax.ShapeDtypeStruct((8 * LEAVES, 128), F32),
        in_specs=[SMEM, SMEM, SMEM, VMEM, HBM, VMEM],
        out_specs=VMEM,
        scratch_shapes=[
            pltpu.VMEM((16, 2, 128, 256), BF16),
            pltpu.VMEM((16, 128), F32),
            pltpu.VMEM((16, 128), F32),
            pltpu.VMEM((128, 128), F32),
            pltpu.VMEM((128, 128), F32),
            pltpu.SemaphoreType.DMA((16,)),
        ],
        compiler_params=pltpu.CompilerParams(vmem_limit_bytes=24 * 2**20),
        name="down",
    )(device, top_list, top_ops, pieces, far_ops, ops)


def far_kernel(index, device, own, *rest):
    ghosts, (far_ops, down, out), scratch = rest[:SLOTS], rest[SLOTS : SLOTS + 3], rest[SLOTS + 3 :]
    first, second, weights, low, high, a0, a1, b0, b1, f0, f1, sems = scratch
    blocks = LEAVES // LB
    groups = OFFS // OG
    steps = blocks * groups

    def fetch(g):
        at = pl.ds(g * OG, OG)
        return pltpu.make_async_copy(far_ops.at[at], weights.at[at], sems.at[g])

    for g in range(groups):
        fetch(g).start()

    def put(row, x):
        size = x.shape[0]
        at = pl.ds(pl.multiple_of(row, size), size)
        first[at, :] = x
        second[at, :] = pltpu.roll(x.reshape(-1, 8, 128), 4, 1).reshape(size, 128)

    @pl.loop(0, LEAVES // 16)
    def _(i):
        put(i * 128, own[pl.ds(pl.multiple_of(i * 128, 128), 128), :].astype(F32))

    last = lax.axis_size("morton")
    for j in range(SLOTS):
        q = device[0] - REACH[j]
        inside = jnp.logical_and(q >= 0, q < last)

        @pl.loop(0, CAP // 16)
        def _(i):
            x = ghosts[j][pl.ds(pl.multiple_of(i * 128, 128), 128), :].astype(F32)
            x = jnp.where(jnp.full(x.shape, inside), x, 0.0)
            put((LEAVES + j * CAP) * 8 + i * 128, x)

    put(EMPTY * 8, jnp.zeros((8, 128), F32))
    low[...] = jnp.zeros_like(low)
    high[...] = jnp.zeros_like(high)
    upper = lax.broadcasted_iota(jnp.int32, (8, 128), 0) < 4

    def gather(s, x0, x1):
        view = index.at[pl.ds(pl.multiple_of(s * (LB * OG), LB * OG), LB * OG)]

        def row(leaf, o):
            return pl.ds(pl.multiple_of(view[leaf * OG + o], 8), 8)

        for i in range(LB // 4):
            for o in range(OG):
                lower = []
                higher = []
                for leaf in (4 * i, 4 * i + 2):
                    v = first[row(leaf, o), :]
                    w = second[row(leaf + 1, o), :]
                    lower.append(jnp.where(upper, v, w))
                    higher.append(jnp.where(upper, w, v))
                at = (pl.ds(16 * i, 16), pl.ds(128 * o, 128))
                x0[at] = jnp.concatenate(lower, axis=0).astype(BF16)
                x1[at] = jnp.concatenate(higher, axis=0).astype(BF16)

    def multiply(s, h, x, total):
        at = pl.ds(pl.multiple_of(s % blocks * (LB * 4), LB * 4), LB * 4)
        w = weights[pl.ds(s // blocks * OG, OG), h].reshape(OG * 128, 256)
        total[at, :] = total[at, :] + dot(x[...], w)

    gather(0, a0, a1)
    for g in range(groups):
        fetch(g).wait()

    @pl.loop(0, steps // 2)
    def _(t):
        multiply(2 * t, 0, a0, low)
        multiply(2 * t, 1, a1, high)
        gather(2 * t + 1, b0, b1)
        multiply(2 * t + 1, 0, b0, low)
        multiply(2 * t + 1, 1, b1, high)
        gather(jnp.minimum(2 * t + 2, steps - 1), a0, a1)

    @pl.loop(0, 16)
    def _(i):
        at = pl.ds(pl.multiple_of(i * 64, 64), 64)
        swapped = pltpu.roll(high[at, :].reshape(8, 8, 256), 4, 1).reshape(64, 256)
        total = low[at, :] + swapped
        f0[at, :] = total[:, :128]
        f1[at, :] = total[:, 128:]

    for k in range(4):
        for h, half in enumerate((f0, f1)):
            for i in range(4):
                far = half[pl.ds(k + 256 * i, 64, stride=4), :]
                near = down[pl.ds((4 * h + k) * LEAVES + 64 * i, 64), :]
                out[pl.ds(64 * i, 64), pl.ds(256 * k + 128 * h, 128)] = near + far


def far_call(index, device, own, ghosts, far_ops, down):
    return pl.pallas_call(
        far_kernel,
        out_shape=jax.ShapeDtypeStruct((LEAVES, 1024), F32),
        in_specs=[SMEM, SMEM] + [VMEM] * (1 + SLOTS) + [HBM, VMEM],
        out_specs=VMEM,
        scratch_shapes=[pltpu.VMEM(((EMPTY + 1) * 8, 128), F32)] * 2
        + [pltpu.VMEM((OFFS, 2, 128, 256), BF16)]
        + [pltpu.VMEM((LEAVES * 4, 256), F32)] * 2
        + [pltpu.VMEM((LB * 4, OG * 128), BF16)] * 4
        + [pltpu.VMEM((LEAVES * 4, 128), F32)] * 2
        + [pltpu.SemaphoreType.DMA((OFFS // OG,))],
        compiler_params=params(52),
        name="far",
    )(index, device, own, *ghosts, far_ops, down)


def shifted(block, distance):
    devices = lax.axis_size("morton")
    route = [((i - distance) % devices, i) for i in range(devices)]
    return lax.ppermute(block, "morton", route)


def shards(charges, basis, m2m_ops, l2l_ops, m2l_ops, send_rows, vlist, top_list, top_ops):
    devices = lax.axis_size("morton")
    device = lax.axis_index("morton").astype(jnp.int32).reshape(1)
    far_ops = m2l_ops.reshape(OFFS, 2, 128, 256)
    own, *packed = leaf_call(send_rows[0], charges, basis.reshape(LEAVES * 64, 256))
    ghosts = [shifted(block, by) for block, by in zip(packed, REACH)]
    piece = up_call(device, own, m2m_ops)
    pieces = lax.all_to_all(
        jnp.broadcast_to(piece[None], (devices, 8, 128)), "morton", 0, 0, tiled=True
    )
    down = down_call(device, top_list, top_ops, pieces, far_ops, l2l_ops)
    index = (vlist * 8).reshape(LEAVES // LB, LB, OFFS // OG, OG)
    index = index.transpose(2, 0, 1, 3).reshape(-1)
    return far_call(index, device, own, ghosts, far_ops, down)


def solution(mesh):
    return jax.shard_map(
        shards,
        mesh=mesh,
        in_specs=(
            P("morton", None),
            P("morton", None, None),
            P(),
            P(),
            P(),
            P("morton", None, None),
            P("morton", None),
            P(),
            P(),
        ),
        out_specs=P("morton", None),
        check_vma=False,
    )
```

```python
import functools

import jax
import jax.numpy as jnp
from jax import lax
from jax.experimental import pallas as pl
from jax.experimental.pallas import tpu as pltpu
from jax.sharding import PartitionSpec as P


F32 = jnp.float32
BF16 = jnp.bfloat16
VMEM = pl.BlockSpec(memory_space=pltpu.VMEM)
SMEM = pl.BlockSpec(memory_space=pltpu.SMEM)
HBM = pl.BlockSpec(memory_space=pl.ANY)

LEAVES = 256
SLOTS = 8
CAP = 128
OFFS = 64
EMPTY = LEAVES + SLOTS * CAP
STEP = 32
LB = 128
OG = 8


BIT = (2, 3, 1, 0)


def climbs(device, j):
    return lax.rem(lax.shift_right_logical(device, BIT[j // 2]), 2) == j % 2


def params(mib):
    return pltpu.CompilerParams(vmem_limit_bytes=mib * 2**20)


def parts(x):
    high = x.astype(BF16)
    low = (x - high.astype(F32)).astype(BF16)
    return jnp.concatenate([high, low], axis=0)


def dot(a, b):
    return jnp.dot(a, b, preferred_element_type=F32)


def leaf_kernel(device, rows, charges, basis, own, *rest):
    packed, (spread0, spread1, table) = rest[:SLOTS], rest[SLOTS:]
    step = pl.program_id(0)

    @pl.when(step == 0)
    def _():
        source = lax.broadcasted_iota(jnp.int32, (256, 256), 0)
        lane = lax.broadcasted_iota(jnp.int32, (256, 256), 1)
        for k in range(4):
            repeat = jnp.where(source == k * 64 + lane % 64, 1.0, 0.0).astype(BF16)
            wide = dot(charges[...], repeat)
            spread0[pl.ds(k, LEAVES, stride=4), :] = wide[:, :128]
            spread1[pl.ds(k, LEAVES, stride=4), :] = wide[:, 128:]

    row = lax.broadcasted_iota(jnp.int32, (16, 256), 0)
    lane = lax.broadcasted_iota(jnp.int32, (16, 256), 1)
    own_block = row // 4 == lane // 64
    upper = lax.broadcasted_iota(jnp.int32, (2, 8, 128), 1) < 4
    for g in range(STEP // 4):
        at = pl.ds(pl.multiple_of(step * (STEP * 4) + 16 * g, 16), 16)
        wide = jnp.concatenate([spread0[at, :], spread1[at, :]], axis=1)
        lhs = jnp.where(own_block, wide, 0.0).astype(BF16)
        res = dot(lhs, basis[256 * g : 256 * g + 256, :])
        x0 = res[:, :128].reshape(2, 8, 128)
        x1 = res[:, 128:].reshape(2, 8, 128)
        even = jnp.where(upper, x0, pltpu.roll(x1, 4, 1))
        odd = jnp.where(upper, pltpu.roll(x0, 4, 1), x1)
        tiles = jnp.concatenate([even[0], odd[0], even[1], odd[1]], axis=0)
        at = pl.ds(pl.multiple_of(step * (STEP * 8) + 32 * g, 32), 32)
        table[at, :] = tiles
        own[at, :] = tiles.astype(BF16)

    @pl.when(step == LEAVES // STEP - 1)
    def _():
        for j in range(SLOTS):
            slot = BIT[j // 2] * 2 + jnp.where(climbs(device[0], j), 0, 1)
            view = rows.at[pl.ds(slot * CAP, CAP)]
            for c in range(0, CAP, 2):
                pair = [table[pl.ds(pl.multiple_of(view[c + d] * 8, 8), 8), :] for d in range(2)]
                packed[j][8 * c : 8 * c + 16, :] = jnp.concatenate(pair, axis=0).astype(BF16)


def leaf_call(device, rows, charges, basis):
    tiles = jax.ShapeDtypeStruct((LEAVES * 8, 128), BF16)
    sent = jax.ShapeDtypeStruct((CAP * 8, 128), BF16)
    whole = lambda i: (0, 0)
    return pl.pallas_call(
        leaf_kernel,
        grid=(LEAVES // STEP,),
        out_shape=[tiles] + [sent] * SLOTS,
        in_specs=[
            SMEM,
            SMEM,
            pl.BlockSpec((LEAVES, 256), whole),
            pl.BlockSpec((STEP * 64, 256), lambda i: (i, 0)),
        ],
        out_specs=[pl.BlockSpec((LEAVES * 8, 128), whole)]
        + [pl.BlockSpec((CAP * 8, 128), whole)] * SLOTS,
        scratch_shapes=[
            pltpu.VMEM((LEAVES * 4, 128), F32),
            pltpu.VMEM((LEAVES * 4, 128), F32),
            pltpu.VMEM((LEAVES * 8, 128), F32),
        ],
        compiler_params=params(60),
        name="leaf",
    )(device, rows, charges, basis)


def up_kernel(device, own, ops, out, wide, p0, p1, g0, g1, lhs, lhs2, tile):
    wide[...] = own[...].astype(F32)
    for c in range(8):
        for h in range(2):
            for k in range(4):
                block = wide[pl.ds(8 * c + 4 * h + k, 32, stride=64), :]
                lhs[32 * k : 32 * k + 32, 256 * c + 128 * h : 256 * c + 128 * h + 128] = block.astype(BF16)
    total = dot(lhs[...], ops[...].reshape(2048, 256))
    p0[...] = total[:, :128]
    p1[...] = total[:, 128:]
    for c in range(8):
        at = pl.ds(c, 16, stride=8)
        lhs2[:, 256 * c : 256 * c + 256] = parts(jnp.concatenate([p0[at, :], p1[at, :]], axis=1))
    total = dot(lhs2[...], ops[...].reshape(2048, 256))
    total = total[:16] + total[16:]
    child = lax.broadcasted_iota(jnp.int32, (16, 256), 0) % 4
    for g in range(4):
        lhs2[:, 256 * g : 256 * g + 256] = parts(jnp.where(child == g, total, 0.0))
    octant = lax.rem(device[0], 2) * 4
    spread = dot(lhs2[:, :1024], ops[pl.ds(octant, 4)].reshape(1024, 256))
    spread = spread[:16] + spread[16:]
    g0[...] = spread[:, :128]
    g1[...] = spread[:, 128:]
    for h, half in enumerate((g0, g1)):
        piece = [half[pl.ds(g, 4, stride=4), :] for g in range(4)]
        tile[4 * h : 4 * h + 4, :] = (piece[0] + piece[1]) + (piece[2] + piece[3])
    out[...] = jnp.broadcast_to(tile[...][None], out.shape)


def up_call(devices, device, own, ops):
    return pl.pallas_call(
        up_kernel,
        out_shape=jax.ShapeDtypeStruct((devices, 8, 128), F32),
        in_specs=[SMEM, VMEM, VMEM],
        out_specs=VMEM,
        scratch_shapes=[
            pltpu.VMEM((LEAVES * 8, 128), F32),
            pltpu.VMEM((128, 128), F32),
            pltpu.VMEM((128, 128), F32),
            pltpu.VMEM((16, 128), F32),
            pltpu.VMEM((16, 128), F32),
            pltpu.VMEM((128, 2048), BF16),
            pltpu.VMEM((32, 2048), BF16),
            pltpu.VMEM((8, 128), F32),
        ],
        compiler_params=params(57),
        name="up",
    )(device, own, ops)


def down_kernel(
    device, top_list, top_ops, pieces, far_ops, ops, out, chosen, lhs, g0, g1, p0, p1, sem
):
    cell = device[0] // 2

    def fetch(e):
        return pltpu.make_async_copy(far_ops.at[top_ops[e, cell]], chosen.at[:, e], sem.at[e])

    for e in range(16):
        fetch(e).start()
    for e in range(16):
        t = top_list[e, cell]
        lhs[:, 128 * e : 128 * e + 128] = parts(pieces[2 * t] + pieces[2 * t + 1])
    for e in range(16):
        fetch(e).wait()
    low = dot(lhs[...], chosen[0].reshape(2048, 256))
    high = dot(lhs[...], chosen[1].reshape(2048, 256))
    top = low[:8] + low[8:] + pltpu.roll(high[:8] + high[8:], 4, 0)
    top = parts(top)
    octant = lax.rem(device[0], 2) * 4
    for g in range(4):
        res = dot(top, ops[octant + g])
        res = res[:8] + res[8:]
        g0[pl.ds(g, 4, stride=4), :] = res[:4, :128]
        g1[pl.ds(g, 4, stride=4), :] = res[:4, 128:]
    grand = parts(jnp.concatenate([g0[...], g1[...]], axis=1))
    for c in range(8):
        res = dot(grand, ops[c])
        res = res[:16] + res[16:]
        p0[pl.ds(c, 16, stride=8), :] = res[:, :128]
        p1[pl.ds(c, 16, stride=8), :] = res[:, 128:]
    parent = parts(jnp.concatenate([p0[...], p1[...]], axis=1))
    for c in range(8):
        res = dot(parent, ops[c])
        res = res[:128] + res[128:]
        for k in range(4):
            for h in range(2):
                at = pl.ds((4 * h + k) * LEAVES + c, 32, stride=8)
                out[at, :] = res[32 * k : 32 * k + 32, 128 * h : 128 * h + 128]


def down_call(device, top_list, top_ops, pieces, far_ops, ops):
    return pl.pallas_call(
        down_kernel,
        out_shape=jax.ShapeDtypeStruct((8 * LEAVES, 128), F32),
        in_specs=[SMEM, SMEM, SMEM, VMEM, HBM, VMEM],
        out_specs=VMEM,
        scratch_shapes=[
            pltpu.VMEM((2, 16, 128, 256), BF16),
            pltpu.VMEM((16, 2048), BF16),
            pltpu.VMEM((16, 128), F32),
            pltpu.VMEM((16, 128), F32),
            pltpu.VMEM((128, 128), F32),
            pltpu.VMEM((128, 128), F32),
            pltpu.SemaphoreType.DMA((16,)),
        ],
        compiler_params=params(57),
        name="down",
    )(device, top_list, top_ops, pieces, far_ops, ops)


def far_kernel(steps_of, index, device, own, *rest):
    ghosts, (far_ops, down, out), scratch = rest[:SLOTS], rest[SLOTS : SLOTS + 3], rest[SLOTS + 3 :]
    first, second, weights, low, high, a0, a1, b0, b1, f0, f1, sems = scratch
    blocks = LEAVES // LB
    groups = OFFS // OG
    steps = blocks * groups


    def fetch(g):
        at = pl.ds(g * OG, OG)
        return pltpu.make_async_copy(far_ops.at[at], weights.at[at], sems.at[g])

    for g in range(groups):
        fetch(g).start()

    def put(row, x):
        size = x.shape[0]
        at = pl.ds(pl.multiple_of(row, size), size)
        first[at, :] = x
        second[at, :] = pltpu.roll(x.reshape(-1, 8, 128), 4, 1).reshape(size, 128)

    @pl.loop(0, LEAVES // 16)
    def _(i):
        put(i * 128, own[pl.ds(pl.multiple_of(i * 128, 128), 128), :].astype(F32))

    last = lax.axis_size("morton")
    for j in range(SLOTS):
        up = climbs(device[0], j)
        q = device[0] + jnp.where(up, 1, -1) * 2 ** BIT[j // 2]
        inside = jnp.logical_and(q >= 0, q < last)
        slot = BIT[j // 2] * 2 + jnp.where(up, 1, 0)
        top = (LEAVES + slot * CAP) * 8

        @pl.loop(0, CAP // 16)
        def _(i):
            x = ghosts[j][pl.ds(pl.multiple_of(i * 128, 128), 128), :].astype(F32)
            x = jnp.where(jnp.full(x.shape, inside), x, 0.0)
            put(top + i * 128, x)

    put(EMPTY * 8, jnp.zeros((8, 128), F32))
    low[...] = jnp.zeros_like(low)
    high[...] = jnp.zeros_like(high)
    upper = lax.broadcasted_iota(jnp.int32, (8, 128), 0) < 4

    next_leaves, next_offset = steps_of[0], steps_of[1]

    def gather(s, x0, x1):
        start = s * (LB * OG)
        for g in range(LB // 8):
            at = start
            for o in range(OG):
                view = index.at[pl.ds(at, 8)]
                row = [pl.ds(pl.multiple_of(view[c], 8), 8) for c in range(8)]
                for i in range(2):
                    lower = []
                    higher = []
                    for leaf in (4 * i, 4 * i + 2):
                        v = first[row[leaf], :]
                        w = second[row[leaf + 1], :]
                        lower.append(jnp.where(upper, v, w))
                        higher.append(jnp.where(upper, w, v))
                    to = (pl.ds(32 * g + 16 * i, 16), pl.ds(128 * o, 128))
                    x0[to] = jnp.concatenate(lower, axis=0).astype(BF16)
                    x1[to] = jnp.concatenate(higher, axis=0).astype(BF16)
                at = at + next_offset
            start = start + next_leaves

    def multiply(s, h, x, total):
        at = pl.ds(pl.multiple_of(s % blocks * (LB * 4), LB * 4), LB * 4)
        w = weights[pl.ds(s // blocks * OG, OG), h].reshape(OG * 128, 256)
        total[at, :] = total[at, :] + dot(x[...], w)

    gather(0, a0, a1)
    for g in range(groups):
        fetch(g).wait()

    @pl.loop(0, steps // 2)
    def _(t):
        multiply(2 * t, 0, a0, low)
        multiply(2 * t, 1, a1, high)
        gather(2 * t + 1, b0, b1)
        multiply(2 * t + 1, 0, b0, low)
        multiply(2 * t + 1, 1, b1, high)
        gather(jnp.minimum(2 * t + 2, steps - 1), a0, a1)

    @pl.loop(0, 16)
    def _(i):
        at = pl.ds(pl.multiple_of(i * 64, 64), 64)
        swapped = pltpu.roll(high[at, :].reshape(8, 8, 256), 4, 1).reshape(64, 256)
        total = low[at, :] + swapped
        f0[at, :] = total[:, :128]
        f1[at, :] = total[:, 128:]

    for k in range(4):
        for h, half in enumerate((f0, f1)):
            for i in range(4):
                far = half[pl.ds(k + 256 * i, 64, stride=4), :]
                near = down[pl.ds((4 * h + k) * LEAVES + 64 * i, 64), :]
                out[pl.ds(64 * i, 64), pl.ds(256 * k + 128 * h, 128)] = near + far


def far_call(lists, device, own, ghosts, far_ops, down):
    return pl.pallas_call(
        far_kernel,
        out_shape=jax.ShapeDtypeStruct((LEAVES, 1024), F32),
        in_specs=[SMEM, SMEM, SMEM] + [VMEM] * (1 + SLOTS) + [HBM, VMEM],
        out_specs=VMEM,
        scratch_shapes=[pltpu.VMEM(((EMPTY + 1) * 8, 128), F32)] * 2
        + [pltpu.VMEM((OFFS, 2, 128, 256), BF16)]
        + [pltpu.VMEM((LEAVES * 4, 256), F32)] * 2
        + [pltpu.VMEM((LB * 4, OG * 128), BF16)] * 4
        + [pltpu.VMEM((LEAVES * 4, 128), F32)] * 2
        + [pltpu.SemaphoreType.DMA((OFFS // OG,))],
        compiler_params=params(60),
        name="far",
    )(jnp.array([8, LB], jnp.int32), lists, device, own, *ghosts, far_ops, down)


def swapped(block, j):
    devices = lax.axis_size("morton")
    step = 2 ** BIT[j // 2]
    route = []
    for i in range(devices):
        partner = i + step if i // step % 2 == j % 2 else i - step
        route.append((i, partner if 0 <= partner < devices else i))
    return lax.ppermute(block, "morton", route)


def listing(vlist):
    rows = (vlist.T * 8).reshape(OFFS // OG, OG, LEAVES // LB, LB)
    return rows.transpose(0, 2, 1, 3).reshape(-1)


def shards(charges, basis, m2m_ops, l2l_ops, m2l_ops, send_rows, vlist, top_list, top_ops):
    devices = lax.axis_size("morton")
    device = lax.axis_index("morton").astype(jnp.int32).reshape(1)
    far_ops = m2l_ops.reshape(OFFS, 2, 128, 256)
    own, *packed = leaf_call(device, send_rows.reshape(SLOTS * CAP), charges, basis.reshape(LEAVES * 64, 256))
    ghosts = [swapped(block, j) for j, block in enumerate(packed)]
    pieces = up_call(devices, device, own, m2m_ops)
    pieces = lax.all_to_all(pieces, "morton", 0, 0, tiled=True)
    down = down_call(device, top_list.T, top_ops.T, pieces, far_ops, l2l_ops)
    return far_call(listing(vlist), device, own, ghosts, far_ops, down)


def solution(mesh):
    return jax.shard_map(
        shards,
        mesh=mesh,
        in_specs=(
            P("morton", None),
            P("morton", None, None),
            P(),
            P(),
            P(),
            P("morton", None, None),
            P("morton", None),
            P(),
            P(),
        ),
        out_specs=P("morton", None),
        check_vma=False,
    )
```

```python
import functools

import jax
import jax.numpy as jnp
from jax import lax
from jax.experimental import pallas as pl
from jax.experimental.pallas import tpu as pltpu
from jax.sharding import PartitionSpec as P


F32 = jnp.float32
BF16 = jnp.bfloat16
VMEM = pl.BlockSpec(memory_space=pltpu.VMEM)
SMEM = pl.BlockSpec(memory_space=pltpu.SMEM)
HBM = pl.BlockSpec(memory_space=pl.ANY)

LEAVES = 256
SLOTS = 8
CAP = 128
OFFS = 64
EMPTY = LEAVES + SLOTS * CAP
STEP = 128
LB = 128
OG = 8


BIT = (2, 3, 1, 0)


def climbs(device, j):
    return lax.rem(lax.shift_right_logical(device, BIT[j // 2]), 2) == j % 2


def params(mib):
    return pltpu.CompilerParams(vmem_limit_bytes=mib * 2**20)


def parts(x):
    high = x.astype(BF16)
    low = (x - high.astype(F32)).astype(BF16)
    return jnp.concatenate([high, low], axis=0)


def dot(a, b):
    return jnp.dot(a, b, preferred_element_type=F32)


def leaf_kernel(device, rows, charges, basis, own, *rest):
    packed, (spread0, spread1, table) = rest[:SLOTS], rest[SLOTS:]
    step = pl.program_id(0)

    @pl.when(step == 0)
    def _():
        source = lax.broadcasted_iota(jnp.int32, (256, 256), 0)
        lane = lax.broadcasted_iota(jnp.int32, (256, 256), 1)
        for k in range(4):
            repeat = jnp.where(source == k * 64 + lane % 64, 1.0, 0.0).astype(BF16)
            wide = dot(charges[...], repeat)
            spread0[pl.ds(k, LEAVES, stride=4), :] = wide[:, :128]
            spread1[pl.ds(k, LEAVES, stride=4), :] = wide[:, 128:]

    row = lax.broadcasted_iota(jnp.int32, (16, 256), 0)
    lane = lax.broadcasted_iota(jnp.int32, (16, 256), 1)
    own_block = row // 4 == lane // 64
    upper = lax.broadcasted_iota(jnp.int32, (2, 8, 128), 1) < 4
    for g in range(STEP // 4):
        at = pl.ds(pl.multiple_of(step * (STEP * 4) + 16 * g, 16), 16)
        wide = jnp.concatenate([spread0[at, :], spread1[at, :]], axis=1)
        lhs = jnp.where(own_block, wide, 0.0).astype(BF16)
        res = dot(lhs, basis[256 * g : 256 * g + 256, :])
        x0 = res[:, :128].reshape(2, 8, 128)
        x1 = res[:, 128:].reshape(2, 8, 128)
        even = jnp.where(upper, x0, pltpu.roll(x1, 4, 1))
        odd = jnp.where(upper, pltpu.roll(x0, 4, 1), x1)
        tiles = jnp.concatenate([even[0], odd[0], even[1], odd[1]], axis=0)
        at = pl.ds(pl.multiple_of(step * (STEP * 8) + 32 * g, 32), 32)
        table[at, :] = tiles
        own[at, :] = tiles.astype(BF16)

    @pl.when(step == LEAVES // STEP - 1)
    def _():
        for j in range(SLOTS):
            slot = BIT[j // 2] * 2 + jnp.where(climbs(device[0], j), 0, 1)
            view = rows.at[pl.ds(slot * CAP, CAP)]
            for c in range(0, CAP, 2):
                pair = [table[pl.ds(pl.multiple_of(view[c + d] * 8, 8), 8), :] for d in range(2)]
                packed[j][8 * c : 8 * c + 16, :] = jnp.concatenate(pair, axis=0).astype(BF16)


def leaf_call(device, rows, charges, basis):
    tiles = jax.ShapeDtypeStruct((LEAVES * 8, 128), BF16)
    sent = jax.ShapeDtypeStruct((CAP * 8, 128), BF16)
    whole = lambda i: (0, 0)
    return pl.pallas_call(
        leaf_kernel,
        grid=(LEAVES // STEP,),
        out_shape=[tiles] + [sent] * SLOTS,
        in_specs=[
            SMEM,
            SMEM,
            pl.BlockSpec((LEAVES, 256), whole),
            pl.BlockSpec((STEP * 64, 256), lambda i: (i, 0)),
        ],
        out_specs=[pl.BlockSpec((LEAVES * 8, 128), whole)]
        + [pl.BlockSpec((CAP * 8, 128), whole)] * SLOTS,
        scratch_shapes=[
            pltpu.VMEM((LEAVES * 4, 128), F32),
            pltpu.VMEM((LEAVES * 4, 128), F32),
            pltpu.VMEM((LEAVES * 8, 128), F32),
        ],
        compiler_params=params(60),
        name="leaf",
    )(device, rows, charges, basis)


def up_kernel(device, own, ops, out, wide, p0, p1, g0, g1, lhs, lhs2, tile):
    wide[...] = own[...].astype(F32)
    for c in range(8):
        for h in range(2):
            for k in range(4):
                block = wide[pl.ds(8 * c + 4 * h + k, 32, stride=64), :]
                lhs[32 * k : 32 * k + 32, 256 * c + 128 * h : 256 * c + 128 * h + 128] = block.astype(BF16)
    total = dot(lhs[...], ops[...].reshape(2048, 256))
    p0[...] = total[:, :128]
    p1[...] = total[:, 128:]
    for c in range(8):
        at = pl.ds(c, 16, stride=8)
        lhs2[:, 256 * c : 256 * c + 256] = parts(jnp.concatenate([p0[at, :], p1[at, :]], axis=1))
    total = dot(lhs2[...], ops[...].reshape(2048, 256))
    total = total[:16] + total[16:]
    child = lax.broadcasted_iota(jnp.int32, (16, 256), 0) % 4
    for g in range(4):
        lhs2[:, 256 * g : 256 * g + 256] = parts(jnp.where(child == g, total, 0.0))
    octant = lax.rem(device[0], 2) * 4
    spread = dot(lhs2[:, :1024], ops[pl.ds(octant, 4)].reshape(1024, 256))
    spread = spread[:16] + spread[16:]
    g0[...] = spread[:, :128]
    g1[...] = spread[:, 128:]
    for h, half in enumerate((g0, g1)):
        piece = [half[pl.ds(g, 4, stride=4), :] for g in range(4)]
        tile[4 * h : 4 * h + 4, :] = (piece[0] + piece[1]) + (piece[2] + piece[3])
    out[...] = jnp.broadcast_to(tile[...][None], out.shape)


def up_call(devices, device, own, ops):
    return pl.pallas_call(
        up_kernel,
        out_shape=jax.ShapeDtypeStruct((devices, 8, 128), F32),
        in_specs=[SMEM, VMEM, VMEM],
        out_specs=VMEM,
        scratch_shapes=[
            pltpu.VMEM((LEAVES * 8, 128), F32),
            pltpu.VMEM((128, 128), F32),
            pltpu.VMEM((128, 128), F32),
            pltpu.VMEM((16, 128), F32),
            pltpu.VMEM((16, 128), F32),
            pltpu.VMEM((128, 2048), BF16),
            pltpu.VMEM((32, 2048), BF16),
            pltpu.VMEM((8, 128), F32),
        ],
        compiler_params=params(16),
        name="up",
    )(device, own, ops)


def down_kernel(
    device, top_list, top_ops, pieces, far_ops, ops, out, chosen, lhs, g0, g1, p0, p1, sem
):
    cell = device[0] // 2

    def fetch(e):
        return pltpu.make_async_copy(far_ops.at[top_ops[e, cell]], chosen.at[:, e], sem.at[e])

    for e in range(16):
        fetch(e).start()
    for e in range(16):
        t = top_list[e, cell]
        lhs[:, 128 * e : 128 * e + 128] = parts(pieces[2 * t] + pieces[2 * t + 1])
    for e in range(16):
        fetch(e).wait()
    low = dot(lhs[...], chosen[0].reshape(2048, 256))
    high = dot(lhs[...], chosen[1].reshape(2048, 256))
    top = low[:8] + low[8:] + pltpu.roll(high[:8] + high[8:], 4, 0)
    top = parts(top)
    octant = lax.rem(device[0], 2) * 4
    for g in range(4):
        res = dot(top, ops[octant + g])
        res = res[:8] + res[8:]
        g0[pl.ds(g, 4, stride=4), :] = res[:4, :128]
        g1[pl.ds(g, 4, stride=4), :] = res[:4, 128:]
    grand = parts(jnp.concatenate([g0[...], g1[...]], axis=1))
    for c in range(8):
        res = dot(grand, ops[c])
        res = res[:16] + res[16:]
        p0[pl.ds(c, 16, stride=8), :] = res[:, :128]
        p1[pl.ds(c, 16, stride=8), :] = res[:, 128:]
    parent = parts(jnp.concatenate([p0[...], p1[...]], axis=1))
    for c in range(8):
        res = dot(parent, ops[c])
        res = res[:128] + res[128:]
        for k in range(4):
            for h in range(2):
                at = pl.ds((4 * h + k) * LEAVES + c, 32, stride=8)
                out[at, :] = res[32 * k : 32 * k + 32, 128 * h : 128 * h + 128]


def down_call(device, top_list, top_ops, pieces, far_ops, ops):
    return pl.pallas_call(
        down_kernel,
        out_shape=jax.ShapeDtypeStruct((8 * LEAVES, 128), F32),
        in_specs=[SMEM, SMEM, SMEM, VMEM, HBM, VMEM],
        out_specs=VMEM,
        scratch_shapes=[
            pltpu.VMEM((2, 16, 128, 256), BF16),
            pltpu.VMEM((16, 2048), BF16),
            pltpu.VMEM((16, 128), F32),
            pltpu.VMEM((16, 128), F32),
            pltpu.VMEM((128, 128), F32),
            pltpu.VMEM((128, 128), F32),
            pltpu.SemaphoreType.DMA((16,)),
        ],
        compiler_params=params(57),
        name="down",
    )(device, top_list, top_ops, pieces, far_ops, ops)


def far_kernel(steps_of, index, device, own, *rest):
    ghosts, (far_ops, down, out), scratch = rest[:SLOTS], rest[SLOTS : SLOTS + 3], rest[SLOTS + 3 :]
    first, second, weights, low, high, a0, a1, b0, b1, f0, f1, sems = scratch
    blocks = LEAVES // LB
    groups = OFFS // OG
    steps = blocks * groups


    def fetch(g):
        at = pl.ds(g * OG, OG)
        return pltpu.make_async_copy(far_ops.at[at], weights.at[at], sems.at[g])

    for g in range(groups):
        fetch(g).start()

    def put(row, x):
        size = x.shape[0]
        at = pl.ds(pl.multiple_of(row, size), size)
        first[at, :] = x
        second[at, :] = pltpu.roll(x.reshape(-1, 8, 128), 4, 1).reshape(size, 128)

    @pl.loop(0, LEAVES // 16)
    def _(i):
        put(i * 128, own[pl.ds(pl.multiple_of(i * 128, 128), 128), :].astype(F32))

    last = lax.axis_size("morton")
    for j in range(SLOTS):
        up = climbs(device[0], j)
        q = device[0] + jnp.where(up, 1, -1) * 2 ** BIT[j // 2]
        inside = jnp.logical_and(q >= 0, q < last)
        slot = BIT[j // 2] * 2 + jnp.where(up, 1, 0)
        top = (LEAVES + slot * CAP) * 8

        @pl.loop(0, CAP // 16)
        def _(i):
            x = ghosts[j][pl.ds(pl.multiple_of(i * 128, 128), 128), :].astype(F32)
            x = jnp.where(jnp.full(x.shape, inside), x, 0.0)
            put(top + i * 128, x)

    put(EMPTY * 8, jnp.zeros((8, 128), F32))
    low[...] = jnp.zeros_like(low)
    high[...] = jnp.zeros_like(high)
    upper = lax.broadcasted_iota(jnp.int32, (8, 128), 0) < 4

    next_leaves, next_offset = steps_of[0], steps_of[1]

    def gather(s, x0, x1):
        start = s * (LB * OG)
        for g in range(LB // 8):
            at = start
            for o in range(OG):
                view = index.at[pl.ds(at, 8)]
                row = [pl.ds(pl.multiple_of(view[c], 8), 8) for c in range(8)]
                for i in range(2):
                    lower = []
                    higher = []
                    for leaf in (4 * i, 4 * i + 2):
                        v = first[row[leaf], :]
                        w = second[row[leaf + 1], :]
                        lower.append(jnp.where(upper, v, w))
                        higher.append(jnp.where(upper, w, v))
                    to = (pl.ds(32 * g + 16 * i, 16), pl.ds(128 * o, 128))
                    x0[to] = jnp.concatenate(lower, axis=0).astype(BF16)
                    x1[to] = jnp.concatenate(higher, axis=0).astype(BF16)
                at = at + next_offset
            start = start + next_leaves

    def multiply(s, h, x, total):
        at = pl.ds(pl.multiple_of(s % blocks * (LB * 4), LB * 4), LB * 4)
        w = weights[pl.ds(s // blocks * OG, OG), h].reshape(OG * 128, 256)
        total[at, :] = total[at, :] + dot(x[...], w)

    gather(0, a0, a1)
    for g in range(groups):
        fetch(g).wait()

    @pl.loop(0, steps // 2)
    def _(t):
        multiply(2 * t, 0, a0, low)
        multiply(2 * t, 1, a1, high)
        gather(2 * t + 1, b0, b1)
        multiply(2 * t + 1, 0, b0, low)
        multiply(2 * t + 1, 1, b1, high)
        gather(jnp.minimum(2 * t + 2, steps - 1), a0, a1)

    @pl.loop(0, 16)
    def _(i):
        at = pl.ds(pl.multiple_of(i * 64, 64), 64)
        swapped = pltpu.roll(high[at, :].reshape(8, 8, 256), 4, 1).reshape(64, 256)
        total = low[at, :] + swapped
        f0[at, :] = total[:, :128]
        f1[at, :] = total[:, 128:]

    for k in range(4):
        for h, half in enumerate((f0, f1)):
            for i in range(4):
                far = half[pl.ds(k + 256 * i, 64, stride=4), :]
                near = down[pl.ds((4 * h + k) * LEAVES + 64 * i, 64), :]
                out[pl.ds(64 * i, 64), pl.ds(256 * k + 128 * h, 128)] = near + far


def far_call(lists, device, own, ghosts, far_ops, down):
    return pl.pallas_call(
        far_kernel,
        out_shape=jax.ShapeDtypeStruct((LEAVES, 1024), F32),
        in_specs=[SMEM, SMEM, SMEM] + [VMEM] * (1 + SLOTS) + [HBM, VMEM],
        out_specs=VMEM,
        scratch_shapes=[pltpu.VMEM(((EMPTY + 1) * 8, 128), F32)] * 2
        + [pltpu.VMEM((OFFS, 2, 128, 256), BF16)]
        + [pltpu.VMEM((LEAVES * 4, 256), F32)] * 2
        + [pltpu.VMEM((LB * 4, OG * 128), BF16)] * 4
        + [pltpu.VMEM((LEAVES * 4, 128), F32)] * 2
        + [pltpu.SemaphoreType.DMA((OFFS // OG,))],
        compiler_params=params(60),
        name="far",
    )(jnp.array([8, LB], jnp.int32), lists, device, own, *ghosts, far_ops, down)


def swapped(block, j):
    devices = lax.axis_size("morton")
    step = 2 ** BIT[j // 2]
    route = []
    for i in range(devices):
        partner = i + step if i // step % 2 == j % 2 else i - step
        route.append((i, partner if 0 <= partner < devices else i))
    return lax.ppermute(block, "morton", route)


def listing(vlist):
    rows = (vlist.T * 8).reshape(OFFS // OG, OG, LEAVES // LB, LB)
    return rows.transpose(0, 2, 1, 3).reshape(-1)


def shards(charges, basis, m2m_ops, l2l_ops, m2l_ops, send_rows, vlist, top_list, top_ops):
    devices = lax.axis_size("morton")
    device = lax.axis_index("morton").astype(jnp.int32).reshape(1)
    far_ops = m2l_ops.reshape(OFFS, 2, 128, 256)
    own, *packed = leaf_call(device, send_rows.reshape(SLOTS * CAP), charges, basis.reshape(LEAVES * 64, 256))
    ghosts = [swapped(block, j) for j, block in enumerate(packed)]
    pieces = up_call(devices, device, own, m2m_ops)
    pieces = lax.all_to_all(pieces, "morton", 0, 0, tiled=True)
    down = down_call(device, top_list.T, top_ops.T, pieces, far_ops, l2l_ops)
    return far_call(listing(vlist), device, own, ghosts, far_ops, down)


def solution(mesh):
    return jax.shard_map(
        shards,
        mesh=mesh,
        in_specs=(
            P("morton", None),
            P("morton", None, None),
            P(),
            P(),
            P(),
            P("morton", None, None),
            P("morton", None),
            P(),
            P(),
        ),
        out_specs=P("morton", None),
        check_vma=False,
    )
```

```python
import functools

import jax
import jax.numpy as jnp
from jax import lax
from jax.experimental import pallas as pl
from jax.experimental.pallas import tpu as pltpu
from jax.sharding import PartitionSpec as P


F32 = jnp.float32
BF16 = jnp.bfloat16
VMEM = pl.BlockSpec(memory_space=pltpu.VMEM)
SMEM = pl.BlockSpec(memory_space=pltpu.SMEM)
HBM = pl.BlockSpec(memory_space=pl.ANY)

LEAVES = 256
SLOTS = 8
CAP = 128
OFFS = 64
EMPTY = LEAVES + SLOTS * CAP
STEP = 128
LB = 128
OG = 8


BIT = (2, 1, 3, 0)


def climbs(device, j):
    return lax.rem(lax.shift_right_logical(device, BIT[j // 2]), 2) == j % 2


def params(mib):
    return pltpu.CompilerParams(vmem_limit_bytes=mib * 2**20)


def parts(x):
    high = x.astype(BF16)
    low = (x - high.astype(F32)).astype(BF16)
    return jnp.concatenate([high, low], axis=0)


def dot(a, b):
    return jnp.dot(a, b, preferred_element_type=F32)


def leaf_kernel(device, rows, charges, basis, own, *rest):
    packed, (spread0, spread1, table) = rest[:SLOTS], rest[SLOTS:]
    step = pl.program_id(0)

    @pl.when(step == 0)
    def _():
        source = lax.broadcasted_iota(jnp.int32, (256, 256), 0)
        lane = lax.broadcasted_iota(jnp.int32, (256, 256), 1)
        for k in range(4):
            repeat = jnp.where(source == k * 64 + lane % 64, 1.0, 0.0).astype(BF16)
            wide = dot(charges[...], repeat)
            spread0[pl.ds(k, LEAVES, stride=4), :] = wide[:, :128]
            spread1[pl.ds(k, LEAVES, stride=4), :] = wide[:, 128:]

    row = lax.broadcasted_iota(jnp.int32, (16, 256), 0)
    lane = lax.broadcasted_iota(jnp.int32, (16, 256), 1)
    own_block = row // 4 == lane // 64
    upper = lax.broadcasted_iota(jnp.int32, (2, 8, 128), 1) < 4
    for g in range(STEP // 4):
        at = pl.ds(pl.multiple_of(step * (STEP * 4) + 16 * g, 16), 16)
        wide = jnp.concatenate([spread0[at, :], spread1[at, :]], axis=1)
        lhs = jnp.where(own_block, wide, 0.0).astype(BF16)
        res = dot(lhs, basis[256 * g : 256 * g + 256, :])
        x0 = res[:, :128].reshape(2, 8, 128)
        x1 = res[:, 128:].reshape(2, 8, 128)
        even = jnp.where(upper, x0, pltpu.roll(x1, 4, 1))
        odd = jnp.where(upper, pltpu.roll(x0, 4, 1), x1)
        tiles = jnp.concatenate([even[0], odd[0], even[1], odd[1]], axis=0)
        at = pl.ds(pl.multiple_of(step * (STEP * 8) + 32 * g, 32), 32)
        table[at, :] = tiles
        own[at, :] = tiles.astype(BF16)

    @pl.when(step == LEAVES // STEP - 1)
    def _():
        for j in range(SLOTS):
            slot = BIT[j // 2] * 2 + jnp.where(climbs(device[0], j), 0, 1)
            view = rows.at[pl.ds(slot * CAP, CAP)]
            for c in range(0, CAP, 2):
                pair = [table[pl.ds(pl.multiple_of(view[c + d] * 8, 8), 8), :] for d in range(2)]
                packed[j][8 * c : 8 * c + 16, :] = jnp.concatenate(pair, axis=0).astype(BF16)


def leaf_call(device, rows, charges, basis):
    tiles = jax.ShapeDtypeStruct((LEAVES * 8, 128), BF16)
    sent = jax.ShapeDtypeStruct((CAP * 8, 128), BF16)
    whole = lambda i: (0, 0)
    return pl.pallas_call(
        leaf_kernel,
        grid=(LEAVES // STEP,),
        out_shape=[tiles] + [sent] * SLOTS,
        in_specs=[
            SMEM,
            SMEM,
            pl.BlockSpec((LEAVES, 256), whole),
            pl.BlockSpec((STEP * 64, 256), lambda i: (i, 0)),
        ],
        out_specs=[pl.BlockSpec((LEAVES * 8, 128), whole)]
        + [pl.BlockSpec((CAP * 8, 128), whole)] * SLOTS,
        scratch_shapes=[
            pltpu.VMEM((LEAVES * 4, 128), F32),
            pltpu.VMEM((LEAVES * 4, 128), F32),
            pltpu.VMEM((LEAVES * 8, 128), F32),
        ],
        compiler_params=params(60),
        name="leaf",
    )(device, rows, charges, basis)


def up_kernel(device, own, ops, out, wide, p0, p1, g0, g1, lhs, lhs2, tile):
    wide[...] = own[...].astype(F32)
    for c in range(8):
        for h in range(2):
            for k in range(4):
                block = wide[pl.ds(8 * c + 4 * h + k, 32, stride=64), :]
                lhs[32 * k : 32 * k + 32, 256 * c + 128 * h : 256 * c + 128 * h + 128] = block.astype(BF16)
    total = dot(lhs[...], ops[...].reshape(2048, 256))
    p0[...] = total[:, :128]
    p1[...] = total[:, 128:]
    for c in range(8):
        at = pl.ds(c, 16, stride=8)
        lhs2[:, 256 * c : 256 * c + 256] = parts(jnp.concatenate([p0[at, :], p1[at, :]], axis=1))
    total = dot(lhs2[...], ops[...].reshape(2048, 256))
    total = total[:16] + total[16:]
    child = lax.broadcasted_iota(jnp.int32, (16, 256), 0) % 4
    for g in range(4):
        lhs2[:, 256 * g : 256 * g + 256] = parts(jnp.where(child == g, total, 0.0))
    octant = lax.rem(device[0], 2) * 4
    spread = dot(lhs2[:, :1024], ops[pl.ds(octant, 4)].reshape(1024, 256))
    spread = spread[:16] + spread[16:]
    g0[...] = spread[:, :128]
    g1[...] = spread[:, 128:]
    for h, half in enumerate((g0, g1)):
        piece = [half[pl.ds(g, 4, stride=4), :] for g in range(4)]
        tile[4 * h : 4 * h + 4, :] = (piece[0] + piece[1]) + (piece[2] + piece[3])
    out[...] = jnp.broadcast_to(tile[...][None], out.shape)


def up_call(devices, device, own, ops):
    return pl.pallas_call(
        up_kernel,
        out_shape=jax.ShapeDtypeStruct((devices, 8, 128), F32),
        in_specs=[SMEM, VMEM, VMEM],
        out_specs=VMEM,
        scratch_shapes=[
            pltpu.VMEM((LEAVES * 8, 128), F32),
            pltpu.VMEM((128, 128), F32),
            pltpu.VMEM((128, 128), F32),
            pltpu.VMEM((16, 128), F32),
            pltpu.VMEM((16, 128), F32),
            pltpu.VMEM((128, 2048), BF16),
            pltpu.VMEM((32, 2048), BF16),
            pltpu.VMEM((8, 128), F32),
        ],
        compiler_params=params(16),
        name="up",
    )(device, own, ops)


def down_kernel(
    device, top_list, top_ops, pieces, far_ops, ops, out, chosen, lhs, g0, g1, p0, p1, sem
):
    cell = device[0] // 2

    def fetch(e):
        return pltpu.make_async_copy(far_ops.at[top_ops[e, cell]], chosen.at[:, e], sem.at[e])

    for e in range(16):
        fetch(e).start()
    for e in range(16):
        t = top_list[e, cell]
        lhs[:, 128 * e : 128 * e + 128] = parts(pieces[2 * t] + pieces[2 * t + 1])
    for e in range(16):
        fetch(e).wait()
    low = dot(lhs[...], chosen[0].reshape(2048, 256))
    high = dot(lhs[...], chosen[1].reshape(2048, 256))
    top = low[:8] + low[8:] + pltpu.roll(high[:8] + high[8:], 4, 0)
    top = parts(top)
    octant = lax.rem(device[0], 2) * 4
    for g in range(4):
        res = dot(top, ops[octant + g])
        res = res[:8] + res[8:]
        g0[pl.ds(g, 4, stride=4), :] = res[:4, :128]
        g1[pl.ds(g, 4, stride=4), :] = res[:4, 128:]
    grand = parts(jnp.concatenate([g0[...], g1[...]], axis=1))
    for c in range(8):
        res = dot(grand, ops[c])
        res = res[:16] + res[16:]
        p0[pl.ds(c, 16, stride=8), :] = res[:, :128]
        p1[pl.ds(c, 16, stride=8), :] = res[:, 128:]
    parent = parts(jnp.concatenate([p0[...], p1[...]], axis=1))
    for c in range(8):
        res = dot(parent, ops[c])
        res = res[:128] + res[128:]
        for k in range(4):
            for h in range(2):
                at = pl.ds((4 * h + k) * LEAVES + c, 32, stride=8)
                out[at, :] = res[32 * k : 32 * k + 32, 128 * h : 128 * h + 128]


def down_call(device, top_list, top_ops, pieces, far_ops, ops):
    return pl.pallas_call(
        down_kernel,
        out_shape=jax.ShapeDtypeStruct((8 * LEAVES, 128), F32),
        in_specs=[SMEM, SMEM, SMEM, VMEM, HBM, VMEM],
        out_specs=VMEM,
        scratch_shapes=[
            pltpu.VMEM((2, 16, 128, 256), BF16),
            pltpu.VMEM((16, 2048), BF16),
            pltpu.VMEM((16, 128), F32),
            pltpu.VMEM((16, 128), F32),
            pltpu.VMEM((128, 128), F32),
            pltpu.VMEM((128, 128), F32),
            pltpu.SemaphoreType.DMA((16,)),
        ],
        compiler_params=params(57),
        name="down",
    )(device, top_list, top_ops, pieces, far_ops, ops)


def far_kernel(steps_of, index, device, own, *rest):
    ghosts, (far_ops, down, out), scratch = rest[:SLOTS], rest[SLOTS : SLOTS + 3], rest[SLOTS + 3 :]
    first, second, weights, low, high, a0, a1, b0, b1, f0, f1, sems = scratch
    blocks = LEAVES // LB
    groups = OFFS // OG
    steps = blocks * groups


    def fetch(g):
        at = pl.ds(g * OG, OG)
        return pltpu.make_async_copy(far_ops.at[at], weights.at[at], sems.at[g])

    for g in range(groups):
        fetch(g).start()

    def put(row, x):
        size = x.shape[0]
        at = pl.ds(pl.multiple_of(row, size), size)
        first[at, :] = x
        second[at, :] = pltpu.roll(x.reshape(-1, 8, 128), 4, 1).reshape(size, 128)

    @pl.loop(0, LEAVES // 16)
    def _(i):
        put(i * 128, own[pl.ds(pl.multiple_of(i * 128, 128), 128), :].astype(F32))

    last = lax.axis_size("morton")
    for j in range(SLOTS):
        up = climbs(device[0], j)
        q = device[0] + jnp.where(up, 1, -1) * 2 ** BIT[j // 2]
        inside = jnp.logical_and(q >= 0, q < last)
        slot = BIT[j // 2] * 2 + jnp.where(up, 1, 0)
        top = (LEAVES + slot * CAP) * 8

        @pl.loop(0, CAP // 16)
        def _(i):
            x = ghosts[j][pl.ds(pl.multiple_of(i * 128, 128), 128), :].astype(F32)
            x = jnp.where(jnp.full(x.shape, inside), x, 0.0)
            put(top + i * 128, x)

    put(EMPTY * 8, jnp.zeros((8, 128), F32))
    low[...] = jnp.zeros_like(low)
    high[...] = jnp.zeros_like(high)
    upper = lax.broadcasted_iota(jnp.int32, (8, 128), 0) < 4

    next_leaves, next_offset = steps_of[0], steps_of[1]

    def gather(s, x0, x1):
        start = s * (LB * OG)
        for g in range(LB // 8):
            at = start
            for o in range(OG):
                view = index.at[pl.ds(at, 8)]
                row = [pl.ds(pl.multiple_of(view[c], 8), 8) for c in range(8)]
                for i in range(2):
                    lower = []
                    higher = []
                    for leaf in (4 * i, 4 * i + 2):
                        v = first[row[leaf], :]
                        w = second[row[leaf + 1], :]
                        lower.append(jnp.where(upper, v, w))
                        higher.append(jnp.where(upper, w, v))
                    to = (pl.ds(32 * g + 16 * i, 16), pl.ds(128 * o, 128))
                    x0[to] = jnp.concatenate(lower, axis=0).astype(BF16)
                    x1[to] = jnp.concatenate(higher, axis=0).astype(BF16)
                at = at + next_offset
            start = start + next_leaves

    def multiply(s, h, x, total):
        at = pl.ds(pl.multiple_of(s % blocks * (LB * 4), LB * 4), LB * 4)
        w = weights[pl.ds(s // blocks * OG, OG), h].reshape(OG * 128, 256)
        total[at, :] = total[at, :] + dot(x[...], w)

    gather(0, a0, a1)
    for g in range(groups):
        fetch(g).wait()

    @pl.loop(0, steps // 2)
    def _(t):
        multiply(2 * t, 0, a0, low)
        multiply(2 * t, 1, a1, high)
        gather(2 * t + 1, b0, b1)
        multiply(2 * t + 1, 0, b0, low)
        multiply(2 * t + 1, 1, b1, high)
        gather(jnp.minimum(2 * t + 2, steps - 1), a0, a1)

    @pl.loop(0, 16)
    def _(i):
        at = pl.ds(pl.multiple_of(i * 64, 64), 64)
        swapped = pltpu.roll(high[at, :].reshape(8, 8, 256), 4, 1).reshape(64, 256)
        total = low[at, :] + swapped
        f0[at, :] = total[:, :128]
        f1[at, :] = total[:, 128:]

    for k in range(4):
        for h, half in enumerate((f0, f1)):
            for i in range(4):
                far = half[pl.ds(k + 256 * i, 64, stride=4), :]
                near = down[pl.ds((4 * h + k) * LEAVES + 64 * i, 64), :]
                out[pl.ds(64 * i, 64), pl.ds(256 * k + 128 * h, 128)] = near + far


def far_call(lists, device, own, ghosts, far_ops, down):
    return pl.pallas_call(
        far_kernel,
        out_shape=jax.ShapeDtypeStruct((LEAVES, 1024), F32),
        in_specs=[SMEM, SMEM, SMEM] + [VMEM] * (1 + SLOTS) + [HBM, VMEM],
        out_specs=VMEM,
        scratch_shapes=[pltpu.VMEM(((EMPTY + 1) * 8, 128), F32)] * 2
        + [pltpu.VMEM((OFFS, 2, 128, 256), BF16)]
        + [pltpu.VMEM((LEAVES * 4, 256), F32)] * 2
        + [pltpu.VMEM((LB * 4, OG * 128), BF16)] * 4
        + [pltpu.VMEM((LEAVES * 4, 128), F32)] * 2
        + [pltpu.SemaphoreType.DMA((OFFS // OG,))],
        compiler_params=params(60),
        name="far",
    )(jnp.array([8, LB], jnp.int32), lists, device, own, *ghosts, far_ops, down)


def swapped(block, j):
    devices = lax.axis_size("morton")
    step = 2 ** BIT[j // 2]
    route = []
    for i in range(devices):
        partner = i + step if i // step % 2 == j % 2 else i - step
        route.append((i, partner if 0 <= partner < devices else i))
    return lax.ppermute(block, "morton", route)


def listing(vlist):
    rows = (vlist.T * 8).reshape(OFFS // OG, OG, LEAVES // LB, LB)
    return rows.transpose(0, 2, 1, 3).reshape(-1)


def shards(charges, basis, m2m_ops, l2l_ops, m2l_ops, send_rows, vlist, top_list, top_ops):
    devices = lax.axis_size("morton")
    device = lax.axis_index("morton").astype(jnp.int32).reshape(1)
    far_ops = m2l_ops.reshape(OFFS, 2, 128, 256)
    own, *packed = leaf_call(device, send_rows.reshape(SLOTS * CAP), charges, basis.reshape(LEAVES * 64, 256))
    ghosts = [swapped(block, j) for j, block in enumerate(packed)]
    pieces = up_call(devices, device, own, m2m_ops)
    pieces = lax.all_to_all(pieces, "morton", 0, 0, tiled=True)
    down = down_call(device, top_list.T, top_ops.T, pieces, far_ops, l2l_ops)
    return far_call(listing(vlist), device, own, ghosts, far_ops, down)


def solution(mesh):
    return jax.shard_map(
        shards,
        mesh=mesh,
        in_specs=(
            P("morton", None),
            P("morton", None, None),
            P(),
            P(),
            P(),
            P("morton", None, None),
            P("morton", None),
            P(),
            P(),
        ),
        out_specs=P("morton", None),
        check_vma=False,
    )
```
